32 devices in a mesh: lat: 8 (over z, y), orient: 4 (over x, core).
Axes of the slice: x: 2, y: 2, z: 4, core: 2. Of those that a mesh axis runs over, the one named last changes fastest.
Arguments:
- features: bfloat16 [16, 32, 32, 8192], P('orient', None, 'lat'), may hold values from -6 to 6
- mix_weights: bfloat16 [2, 3, 32, 32], replicated, may hold values from -0.625 to 0.625
- kernels: bfloat16 [2, 9, 32, 32], replicated, may hold values from -0.375 to 0.375
- bias_terms: float32 [2, 32], replicated, may hold values from -3 to 3
Outputs:
- responses: bfloat16 [16, 32, 32, 8192], P('orient', None, 'lat')
The draws below stay inside these ranges and needn't reach their ends.
All inputs are finite; a program needn't handle non-finite values.
Results may differ from the reference program's by a relative error of at most 0.0061.
Values may be sent and summed in bfloat16 or wider, within the bound.
No kernel may reach another device: no remote copies, remote signals or barrier semaphores. Data moves between devices by JAX's collectives and lax.ppermute only.
A program may use at most 128 MiB of HBM per device.

```python
import jax
import jax.numpy as jnp
import numpy as np
from jax import lax

ORIENTS = 16
C = 32
W = 8192
LAYERS = 2
ROWS = 32


def steps_of(stream_key, shape, split, smallest, top_value):
    loudness, own = 1.0, jax.random.fold_in(stream_key, 6)
    for dim, parts in split:
        steps = jnp.exp(jax.random.uniform(jax.random.fold_in(own, dim), (parts,), jnp.float32, smallest / len(split), top_value / len(split)))
        loudness = loudness * jnp.repeat(steps, shape[dim] // parts).reshape([-1 if axis == dim else 1 for axis in range(len(shape))])
    return loudness


def scatter_about(stream_key, dims, scale, most, split=(), held_as=jnp.bfloat16):
    loudness = steps_of(stream_key, dims, split, -0.22, 0.18) if split else 1.0
    values = jax.random.normal(stream_key, dims, jnp.float32) * scale * loudness
    return jnp.minimum(jnp.maximum(values, -most), most).astype(held_as)


def setup_inputs(seed: int = 0) -> dict:
    splits = jax.random.split(jax.random.key(seed), 5)
    features = scatter_about(splits[0], (ORIENTS, C, ROWS, W), 1.0, 6.0, ((0, 4), (2, 8)))
    mix_weights = scatter_about(splits[1], (LAYERS, 3, C, C), (3 * C) ** -0.5, 0.625)
    kernels = scatter_about(splits[2], (LAYERS, 9, C, C), (9 * C) ** -0.5, 0.375)
    bias_terms = scatter_about(splits[3], (LAYERS, C), 0.5, 3.0, (), jnp.float32)
    return {"features": features, "mix_weights": mix_weights, "kernels": kernels, "bias_terms": bias_terms}


CYCLE_PLACE = np.array([0, 1, 2, 7, -1, 3, 6, 5, 4])
CYCLE_PAIRS = np.outer((CYCLE_PLACE >= 0).astype(np.float32), (CYCLE_PLACE >= 0).astype(np.float32))
CENTER_ONE = np.outer((CYCLE_PLACE < 0).astype(np.float32), (CYCLE_PLACE < 0).astype(np.float32))


def rotation_table(orient):
    half_turn = orient.astype(jnp.float32) * 0.5
    positions = jnp.asarray(CYCLE_PLACE).astype(jnp.float32)
    distance = jnp.mod(positions[:, None] - positions[None, :] - half_turn + 4.0, 8.0) - 4.0
    weight = jnp.maximum(0.0, 1.0 - jnp.abs(distance))
    return weight * jnp.asarray(CYCLE_PAIRS).astype(jnp.float32) + jnp.asarray(CENTER_ONE).astype(jnp.float32)


def rotated_kernels(kernel, orient):
    table = rotation_table(orient)
    return jnp.einsum("ab,bij->aij", table, kernel.astype(jnp.float32), precision=lax.Precision.HIGHEST).astype(jnp.bfloat16)


def one_layer(current, mixing, kernel, bias_row):
    def per_orient(orient):
        running = jnp.zeros((C, ROWS, W), jnp.float32)
        for offset in range(3):
            source = current[jnp.mod(orient + offset - 1, ORIENTS)]
            running = running + jnp.einsum("ij,jrw->irw", mixing[offset].astype(jnp.float32), source.astype(jnp.float32))
        mixed_feats = running.astype(jnp.bfloat16)
        padded = jnp.pad(mixed_feats, ((0, 0), (1, 1), (0, 0)))
        rotated = rotated_kernels(kernel, orient)
        result = jnp.zeros((C, ROWS, W), jnp.float32)
        for tap_index in range(9):
            row_start = tap_index // 3
            col_shift = tap_index % 3 - 1
            window = jnp.roll(padded[:, row_start:row_start + ROWS, :], -col_shift, axis=2)
            result = result + jnp.einsum("ij,jrw->irw", rotated[tap_index].astype(jnp.float32), window.astype(jnp.float32))
        return jax.nn.relu(result + bias_row[:, None, None]).astype(jnp.bfloat16)

    return lax.map(per_orient, jnp.arange(ORIENTS, dtype=jnp.int32))


def reference(features, mix_weights, kernels, bias_terms):
    current = features
    for layer_index in range(LAYERS):
        current = one_layer(current, mix_weights[layer_index], kernels[layer_index], bias_terms[layer_index])
    return current
```

```python
import functools

import jax
import jax.numpy as jnp
import numpy as np
from jax import lax
from jax.experimental import pallas as pl
from jax.experimental.pallas import tpu as pltpu
from jax.sharding import PartitionSpec as P

LAYERS = 2
EDGE = 128
SHARES = (5, 7, 10, 10)
JOINED = ((0, 1), (2,), (3,))
COST = {"mix": 10**6, "conv": 10**11}
VMEM_BYTES = 20 * 2**20
BF16 = jnp.bfloat16
F32 = jnp.float32

CYCLE = (0, 1, 2, 5, 8, 7, 6, 3)

ANY = pl.BlockSpec(memory_space=pl.ANY)
HBM = pl.BlockSpec(memory_space=pltpu.HBM)
VMEM = pl.BlockSpec(memory_space=pltpu.VMEM)
SMEM = pl.BlockSpec(memory_space=pltpu.SMEM)


def tile_of(length, most):
    blocks = length // EDGE
    return EDGE * max(d for d in range(1, most // EDGE + 1) if blocks % d == 0)


def one_hot(shape, hit):
    first = lax.broadcasted_iota(jnp.int32, shape, 0)
    second = lax.broadcasted_iota(jnp.int32, shape, 1)
    return jnp.where(hit(first, second), 1.0, 0.0).astype(BF16)


def run_copies(copies, sems):
    started = [pltpu.make_async_copy(src, dst, sems.at[i]) for i, (src, dst) in enumerate(copies)]
    for copy in started:
        copy.start()
    for copy in started:
        copy.wait()


def call(body, outs, out_specs, in_specs, scratch, args, aliases=None, cost=1):
    return pl.pallas_call(
        body,
        out_shape=outs,
        in_specs=in_specs,
        out_specs=out_specs,
        scratch_shapes=scratch,
        input_output_aliases=aliases or {},
        cost_estimate=pl.CostEstimate(flops=cost, bytes_accessed=1, transcendentals=0),
        compiler_params=pltpu.CompilerParams(vmem_limit_bytes=VMEM_BYTES),
    )(*args)


def segments(start, stop, width):
    pieces, at = [], start
    while at < stop:
        begin = at % width
        length = min(stop - at, width - begin)
        pieces.append((begin, at - start, length))
        at += length
    return pieces


def mix_weight_body(channels, rows, mix_ref, *out_refs):
    span = channels * rows
    for layer in range(LAYERS):
        for offset in range(3):
            for row in range(rows):
                if layer == 0:
                    place = one_hot((channels, span), lambda c, k: k == c * rows + row)
                else:
                    place = one_hot((channels, span), lambda c, k: k == row * channels + c)
                block = jnp.dot(mix_ref[layer, offset], place, preferred_element_type=F32)
                out_refs[layer][pl.ds(row * channels, channels), pl.ds(offset * span, span)] = block.astype(BF16)


def conv_weight_body(count, channels, rows, first_ref, kernel_ref, *refs):
    out_refs = refs[-LAYERS:]
    span = channels * rows
    depth = channels * (rows + 2)
    swap = one_hot((span, span), lambda a, b: b == (a % rows) * channels + a // rows)
    for here in range(count):
        orient = first_ref[0] + here
        weights = []
        for diff in range(8):
            halves = jnp.bitwise_and(2 * diff - orient + 8, 15) - 8
            weights.append(jnp.maximum(2 - jnp.abs(halves), 0).astype(F32) * 0.5)
        for layer in range(LAYERS):
            taps = [kernel_ref[layer, tap].astype(F32) for tap in range(9)]
            turned = [None] * 9
            turned[4] = taps[4]
            for a in range(8):
                total = None
                for diff in range(8):
                    term = weights[diff] * taps[CYCLE[(a - diff) % 8]]
                    total = term if total is None else total + term
                turned[CYCLE[a]] = total
            turned = jnp.concatenate(turned, axis=0).astype(BF16)
            spread = [
                jnp.dot(
                    turned,
                    one_hot((channels, depth), lambda c, k: k == line * channels + c),
                    preferred_element_type=F32,
                )
                for line in range(rows + 2)
            ]
            for col in range(3):
                blocks = []
                for row in range(rows):
                    total = None
                    for dy in range(3):
                        tap = 3 * dy + col
                        term = spread[row + dy][tap * channels : (tap + 1) * channels]
                        total = term if total is None else total + term
                    blocks.append(total)
                block = jnp.concatenate(blocks, axis=0).astype(BF16)
                if layer == LAYERS - 1:
                    block = jnp.dot(swap, block, preferred_element_type=F32).astype(BF16)
                out_refs[layer][here, pl.ds(col * span, span), :] = block


def edge_copies(pieces, cur_ref, last_ref, first_ref):
    count = cur_ref.shape[0]
    copies = []
    for src, dst, size in pieces:
        source, target = pl.ds(src, size), pl.ds(dst, size)
        copies.append((cur_ref.at[count - 1, ..., source], last_ref.at[..., target]))
        copies.append((cur_ref.at[0, ..., source], first_ref.at[..., target]))
    return copies


def pick_body(pieces, n_deps, cur_ref, *refs):
    last_ref, first_ref, sems = refs[n_deps:]
    run_copies(edge_copies(pieces, cur_ref, last_ref, first_ref), sems)


def mix_body(count, channels, rows, pieces, next_pieces, n_deps, *refs):
    weight_ref, cur_ref, low_ref, high_ref = refs[:4]
    refs = refs[4:]
    if next_pieces:
        next_ref, refs = refs[0], refs[1:]
    refs = refs[n_deps:]
    main_ref, top_ref, bottom_ref = refs[:3]
    refs = refs[3:]
    span = channels * rows
    length = main_ref.shape[-1]
    copies = []
    if next_pieces:
        send_ref, last_ref, first_ref = next_ref, *refs[:2]
        refs = refs[2:]
        copies += edge_copies(next_pieces, send_ref, last_ref, first_ref)
    if pieces is None:
        flat, sems = refs
        copies.append((cur_ref, flat.at[pl.ds(1, count)]))
        copies.append((low_ref, flat.at[0]))
        copies.append((high_ref, flat.at[count + 1]))
    else:
        flat, raw, sems = refs
        for src, dst, size in pieces:
            copies.append((cur_ref.at[:, :, :, pl.ds(src, size)], raw.at[pl.ds(1, count), :, :, pl.ds(dst, size)]))
        copies.append((low_ref, raw.at[0]))
        copies.append((high_ref, raw.at[count + 1]))
    run_copies(copies, sems)
    step = tile_of(length, 1408)

    @pl.loop(0, length // step)
    def _(index):
        cols = pl.ds(pl.multiple_of(index * step, EDGE), step)
        if pieces is not None:
            for slot in range(count + 2):
                flat[slot, :, cols] = raw[slot, :, :, cols].reshape(span, step)
        for here in range(count):
            stack = flat[pl.ds(here, 3), :, cols].reshape(3 * span, step)
            mixed = jnp.dot(weight_ref[...], stack, preferred_element_type=F32).astype(BF16)
            main_ref[here, :, cols] = mixed
            top_ref[here, :, cols] = mixed[:channels]
            bottom_ref[here, :, cols] = mixed[span - channels :]


def conv_body(count, channels, rows, cuts, n_arrays, n_deps, place, *refs):
    weight_ref, bias_ref = refs[:2]
    pieces = refs[2 : 2 + 3 * n_arrays]
    refs = refs[2 + 3 * n_arrays + n_deps :]
    span = channels * rows
    if place is None:
        main_ref, held, sems = refs
    else:
        out_ref, done, held, sems = refs
    length = held.shape[-1] - 2 * EDGE
    copies = []
    for array, src, dst, size in cuts:
        main, top, bottom = pieces[3 * array : 3 * array + 3]
        source, target = pl.ds(src, size), pl.ds(dst, size)
        copies.append((top.at[:, :, source], held.at[:, pl.ds(0, channels), target]))
        copies.append((main.at[:, :, source], held.at[:, pl.ds(channels, span), target]))
        copies.append((bottom.at[:, :, source], held.at[:, pl.ds(channels + span, channels), target]))
    run_copies(copies, sems)
    step = tile_of(length, 1664)

    @pl.loop(0, length // step)
    def _(index):
        begin = pl.multiple_of(index * step, EDGE)
        cols = pl.ds(begin, step)
        for here in range(count):
            block = held[here, :, pl.ds(begin, step + 2 * EDGE)]
            terms = jnp.dot(weight_ref[here], block, preferred_element_type=F32)
            total = (
                pltpu.roll(terms[:span], 1, 1)
                + terms[span : 2 * span]
                + pltpu.roll(terms[2 * span :], step + 2 * EDGE - 1, 1)
            )
            total = jnp.maximum(total[:, EDGE : EDGE + step] + bias_ref[...], 0.0).astype(BF16)
            if place is None:
                main_ref[here, :, cols] = total
            else:
                done[here, :, :, cols] = total.reshape(channels, rows, step)

    if place is not None:
        run_copies([(done, out_ref.at[:, :, :, pl.ds(place, length)])], sems)


def ring(axis, count, periodic):
    forward = [(i, i + 1) for i in range(count - 1)]
    if periodic:
        forward.append((count - 1, 0))
    return (
        lambda block: lax.ppermute(block, axis, forward),
        lambda block: lax.ppermute(block, axis, [(b, a) for a, b in forward]),
    )


def local(sizes, features, mix_weights, kernels, bias_terms):
    count, channels, rows, width = features.shape
    span = channels * rows
    features = pltpu.with_memory_space_constraint(features, pltpu.HBM)
    orient_up, orient_down = ring("orient", sizes["orient"], True)
    lat_up, lat_down = ring("lat", sizes["lat"], False)
    n = len(SHARES)
    shape = jax.ShapeDtypeStruct
    dma = pltpu.SemaphoreType.DMA

    bounds = [-2 * EDGE]
    for share in SHARES:
        bounds.append(bounds[-1] + share * (width // sum(SHARES)))
    ranges = [[(bounds[i], bounds[i + 1]) for i in range(n)]]
    joined = [(bounds[group[0]], bounds[group[-1] + 1]) for group in JOINED]
    for _ in range(LAYERS):
        joined = [(a - EDGE, b - EDGE) for a, b in joined]
        joined[0] = (joined[0][0] + 2 * EDGE, joined[0][1])
        joined[-1] = (joined[-1][0], joined[-1][1] + 2 * EDGE)
        ranges.append(joined)

    first_orient = (lax.axis_index("orient") * count).astype(jnp.int32).reshape(1)
    bias_rows = jnp.tile(bias_terms[: LAYERS - 1], (1, rows))
    bias_last = jnp.repeat(bias_terms[LAYERS - 1 :], rows, axis=1)
    biases = [row[:, None] for row in (*bias_rows, *bias_last)]

    mix_all = call(
        functools.partial(mix_weight_body, channels, rows),
        (shape((span, 3 * span), BF16),) * LAYERS,
        (VMEM,) * LAYERS,
        [VMEM],
        [],
        [mix_weights],
    )

    def edges(layer, index):
        a, b = ranges[layer][index]
        if layer == 0:
            return segments(a, b, width), shape((channels, rows, b - a), BF16)
        return [(0, 0, b - a)], shape((span, b - a), BF16)

    def mix(layer, index, cur, low, high, following, deps):
        a, b = ranges[layer][index]
        length = b - a
        pieces = next_pieces = None
        outs = [shape((count, span, length), BF16)] + [shape((count, channels, length), BF16)] * 2
        specs = [VMEM, VMEM, VMEM]
        scratch = [pltpu.VMEM((count + 2, span, length), BF16)]
        copies = 3
        args = [mix_all[layer], cur, low, high]
        if layer == 0:
            pieces = segments(a, b, width)
            copies = 2 + len(pieces)
            scratch.append(pltpu.VMEM((count + 2, channels, rows, length), BF16))
        if following is not None:
            source, next_layer, next_index = following
            args.append(source)
            next_pieces, block = edges(next_layer, next_index)
            copies += 2 * len(next_pieces)
            outs += [block] * 2
            specs += [VMEM, VMEM]
        scratch.append(dma((copies,)))
        return call(
            functools.partial(mix_body, count, channels, rows, pieces, next_pieces, len(deps)),
            tuple(outs),
            tuple(specs),
            [VMEM] + [ANY] * (len(args) - 1 + len(deps)),
            scratch,
            [*args, *deps],
            cost=COST["mix"],
        )

    def conv(layer, index, weights, held, out=None, deps=()):
        start, stop = ranges[layer + 1][index]
        need = (start - EDGE, stop + EDGE)
        used, cuts = [], []
        for which, (a, b) in enumerate(ranges[layer]):
            for turn in (0, width):
                lo, hi = max(need[0], a + turn), min(need[1], b + turn)
                if lo < hi:
                    if which not in used:
                        used.append(which)
                    cuts.append((used.index(which), lo - a - turn, lo - need[0], hi - lo))
        arrays = [array for which in used for array in held[which]]
        length = stop - start
        scratch = [
            pltpu.VMEM((count, span + 2 * channels, length + 2 * EDGE), BF16),
            dma((3 * len(cuts),)),
        ]
        aliases = {}
        deps = list(deps)
        if layer < LAYERS - 1:
            place = None
            outs = shape((count, span, length), BF16)
            specs = VMEM
        else:
            place = start
            outs = shape(features.shape, BF16)
            specs = ANY
            scratch.insert(0, pltpu.VMEM((count, channels, rows, length), BF16))
            if out is not None:
                aliases = {2 + len(arrays): 0}
                deps = [out] + deps
        return call(
            functools.partial(conv_body, count, channels, rows, cuts, len(used), len(deps), place),
            outs,
            specs,
            [VMEM, VMEM] + [ANY] * (len(arrays) + len(deps)),
            scratch,
            [weights[layer], biases[layer], *arrays, *deps],
            aliases,
            cost=COST["conv"],
        )

    stages = [(layer, index) for layer in range(LAYERS) for index in range(len(ranges[layer]))]
    current = {(0, index): features for index in range(n)}
    held = [[None] * len(ranges[layer]) for layer in range(LAYERS)]

    def pick(index, deps):
        pieces, block = edges(0, index)
        return call(
            functools.partial(pick_body, pieces, len(deps)),
            (block, block),
            (VMEM, VMEM),
            [ANY] * (1 + len(deps)),
            [dma((2 * len(pieces),))],
            [features, *deps],
        )

    def gate(pair, deps):
        return call(
            lambda *refs: None,
            tuple(shape(block.shape, BF16) for block in pair),
            (ANY, ANY),
            [ANY] * (2 + len(deps)),
            [],
            [*pair, *deps],
            {0: 0, 1: 1},
        )

    def send(pair):
        return orient_up(pair[0]), orient_down(pair[1])

    sent = pick(0, ())
    arrived = [send(sent)]
    second = pick(1, (*sent, *mix_all, *biases))
    arrived.append(send(gate(second, arrived[0])))
    weights = out = None
    token = ()
    finished = {group[-1]: index for index, group in enumerate(JOINED)}

    for stage in range(len(stages) + 1):
        if stage < len(stages):
            layer, index = stages[stage]
            low, high = arrived[stage]
            following = None
            if 1 <= stage < len(stages) - 1:
                following = (current[stages[stage + 1]], *stages[stage + 1])
            got = mix(layer, index, current[layer, index], low, high, following, token)
            edge_rows = got[1:3]
            if stage == 1:
                edge_rows = gate(edge_rows, held[0][0][1:])
            held[layer][index] = (got[0], lat_up(edge_rows[1]), lat_down(edge_rows[0]))
            if following is not None:
                arrived.append(send(got[3:]))
            token = (edge_rows[0],)
        if stage == 0:
            continue
        layer, index = stages[stage - 1]
        if layer == 0 and index not in finished:
            if weights is None:
                deps = token
                weights = call(
                    functools.partial(conv_weight_body, count, channels, rows),
                    (shape((count, 3 * span, span + 2 * channels), BF16),) * LAYERS,
                    (VMEM,) * LAYERS,
                    [SMEM, VMEM] + [ANY] * len(deps),
                    [],
                    [first_orient, kernels, *deps],
                    cost=COST["conv"],
                )
                token = (weights[0],)
        elif layer == 0:
            got = conv(layer, finished[index], weights, held[layer], out, token)
            current[layer + 1, finished[index]] = got
            token = (got,)
        else:
            out = conv(layer, index, weights, held[layer], out, token)
            token = ()
    return out


def solution(mesh):
    spec = P("orient", None, "lat", None)
    return jax.shard_map(
        functools.partial(local, dict(mesh.shape)),
        mesh=mesh,
        in_specs=(spec, P(), P(), P()),
        out_specs=spec,
        check_vma=False,
    )
```
